256 devices in a mesh: dp: 32 (over z, y), tensor: 8 (over x, core).
Axes of the slice: x: 4, y: 4, z: 8, core: 2. Of those that a mesh axis runs over, the one named last changes fastest.
Arguments:
- activations: bfloat16 [8192, 8192], P('dp'), may hold values from -6 to 6
- out_grads: bfloat16 [8192, 4096], P('dp', 'tensor'), may hold values from -0.25 to 0.25
- owner: int32 [8, 16], P('tensor'), may hold values from 0 to 31, as said below
- slot: int32 [8, 16], P('tensor'), may hold values from 0 to 1, as said below
- left_state: float32 [8, 32, 2, 512, 512], P('tensor', 'dp'), as said below
- right_state: float32 [8, 32, 2, 512, 512], P('tensor', 'dp'), as said below
Outputs:
- direction: bfloat16 [8192, 4096], P('dp', 'tensor')
- left_out: float32 [8, 32, 2, 512, 512], P('tensor', 'dp')
- right_out: float32 [8, 32, 2, 512, 512], P('tensor', 'dp')
The draws below stay inside these ranges and needn't reach their ends.
Inputs may be any that keep to these rules, and one draw needn't show every extreme that they name: For each index of tensor, at most 2 blocks share an owner and some owner holds exactly 2; no two blocks share an owner and a slot. `slot`: together with owner, distinct for all blocks of one index of tensor. `left_state`: symmetric and diagonally dominant with positive diagonal. `right_state`: symmetric and diagonally dominant with positive diagonal.
All inputs are finite; a program needn't handle non-finite values.
Results may differ from the reference program's by a relative error of at most 0.025.
Values may be sent and summed in bfloat16 or wider, within the bound.
A program may use at most 128 MiB of HBM per device.

```python
import jax
import jax.numpy as jnp
from jax import lax

D = 8192
BLOCK_ORDER = 512
ITERS = 2
TOK_DEV = 256
TOKENS = 8192
COLS = 4096
NBR = 16
NBC = 1
NBLK = 16
SLOTS = 2
N_DP = 32
N_TENSOR = 8


def assignment(key):
    cells = N_DP * SLOTS

    def one_row(row_key):
        key_busy, key_rest, key_order = jax.random.split(row_key, 3)
        busy = jax.random.randint(key_busy, (), 0, N_DP)
        rest = jax.random.permutation(key_rest, cells - SLOTS).astype(jnp.int32)
        rest = jnp.where(rest < busy * SLOTS, rest, rest + SLOTS)
        chosen = jnp.concatenate([busy * SLOTS + jnp.arange(SLOTS, dtype=jnp.int32), rest[:NBLK - SLOTS]])
        order = jax.random.permutation(key_order, NBLK)
        return jnp.zeros((NBLK,), jnp.int32).at[order].set(chosen)
    placed = jax.vmap(one_row)(jax.random.split(key, N_TENSOR))
    return (placed // SLOTS, placed % SLOTS)


def statistics(key, widest):
    key_off, key_diag, key_scale = jax.random.split(key, 3)
    gradient_shape = (N_TENSOR, N_DP, SLOTS, BLOCK_ORDER, BLOCK_ORDER)
    raw = jax.random.uniform(key_off, gradient_shape, jnp.float32, -1.0, 1.0)
    sym = 0.125 * (raw + jnp.swapaxes(raw, -1, -2))
    eye = jnp.eye(BLOCK_ORDER, dtype=jnp.float32)
    diag = jax.random.uniform(key_diag, gradient_shape[:-1], jnp.float32, 1.2, 2.4) * (BLOCK_ORDER - 1) * 0.25
    mat = sym * (1.0 - eye) + eye * diag[..., :, None]
    scales = jnp.exp(jax.random.uniform(key_scale, gradient_shape[:-1], jnp.float32, 0.0, jnp.log(widest)))
    return mat * scales[..., :, None] * scales[..., None, :]


def draw_owner(key, part):
    shared = assignment(key)
    return shared[0]


def draw_slot(key, part):
    shared = assignment(key)
    return shared[1]


def draw_left_state(key, part):
    key = jax.random.fold_in(key, 5)
    return statistics(key, 3.0)


def draw_right_state(key, part):
    key = jax.random.fold_in(key, 6)
    return statistics(key, 3.0)


def steps_of(rng, extent, cuts, low, largest):
    loudness, own = 1.0, jax.random.fold_in(rng, 6)
    for dim, shards_of in cuts:
        steps = jnp.exp(jax.random.uniform(jax.random.fold_in(own, dim), (shards_of,), jnp.float32, low / len(cuts), largest / len(cuts)))
        loudness = loudness * jnp.repeat(steps, extent[dim] // shards_of).reshape([-1 if axis == dim else 1 for axis in range(len(extent))])
    return loudness


def noise(stream_key, shape, width, most, cuts=(), kind=jnp.bfloat16):
    level = steps_of(stream_key, shape, cuts, -0.22, 0.18) if cuts else 1.0
    values = jax.random.normal(stream_key, shape, jnp.float32) * width * level
    return jnp.minimum(jnp.maximum(values, -most), most).astype(kind)


def setup_inputs(seed: int = 0) -> dict:
    keys = jax.random.split(jax.random.key(seed), 7)
    activations = noise(keys[0], (TOKENS, D), 1.0, 6.0, ((0, 32),))
    out_grads = noise(keys[1], (TOKENS, COLS), 0.015625, 0.25, ((0, 32), (1, 8)))
    owner = draw_owner(jax.random.fold_in(keys[6], 71), 0)
    slot = draw_slot(jax.random.fold_in(keys[6], 71), 0)
    left_state = draw_left_state(jax.random.fold_in(keys[6], 71), 0)
    right_state = draw_right_state(jax.random.fold_in(keys[6], 71), 0)
    return dict(activations=activations, out_grads=out_grads, owner=owner, slot=slot, left_state=left_state, right_state=right_state)


BETA = 0.95

def matrix_multiply(left, right):
    return jnp.matmul(left, right, precision=lax.Precision.HIGHEST)

def inverse_root(mat):
    eye = jnp.eye(mat.shape[-1], dtype=jnp.float32)
    norm = jnp.sqrt(lax.optimization_barrier(jnp.sum(mat * mat, axis=(-2, -1), keepdims=True)))
    scale = 5.0 / (2.0 * norm)
    mat_m = mat * scale
    root = eye * scale ** 0.25
    for step in range(ITERS):
        step_m = 1.25 * eye - 0.25 * mat_m
        root = matrix_multiply(root, step_m)
        if step + 1 < ITERS:
            square = matrix_multiply(step_m, step_m)
            mat_m = matrix_multiply(matrix_multiply(square, square), mat_m)
    return root

def reference(activations, out_grads, owner, slot, left_state, right_state):
    acts = activations.reshape(N_DP, TOK_DEV, D)
    outs = out_grads.reshape(N_DP, TOK_DEV, COLS)

    def add_part(carry, pair):
        term = jnp.dot(pair[0].T, pair[1], preferred_element_type=jnp.float32)
        rounded = lax.optimization_barrier(term.astype(jnp.bfloat16)).astype(jnp.float32)
        return (carry + rounded, None)
    total, _ = lax.scan(add_part, jnp.zeros((D, COLS), jnp.float32), (acts, outs))
    grad = total.astype(jnp.bfloat16)
    blocks = grad.astype(jnp.float32).reshape(NBR, BLOCK_ORDER, N_TENSOR, NBC, BLOCK_ORDER)
    blocks = blocks.transpose(2, 0, 3, 1, 4).reshape(N_TENSOR, NBLK, BLOCK_ORDER, BLOCK_ORDER)
    tens = jnp.arange(N_TENSOR, dtype=jnp.int32)[:, None]
    left_previous = left_state[tens, owner, slot]
    right_old = right_state[tens, owner, slot]

    def per_tensor(group):
        gradient_blocks, left_prev, right_prev = group
        left_new = BETA * left_prev + jnp.einsum('bij,bkj->bik', gradient_blocks, gradient_blocks, precision=lax.Precision.HIGHEST)
        right_new = BETA * right_prev + jnp.einsum('bji,bjk->bik', gradient_blocks, gradient_blocks, precision=lax.Precision.HIGHEST)
        preconditioned_update = matrix_multiply(matrix_multiply(inverse_root(left_new), gradient_blocks), inverse_root(right_new))
        return (left_new, right_new, preconditioned_update.astype(jnp.bfloat16))
    left_new, right_new, pre = lax.map(per_tensor, (blocks, left_previous, right_old))
    grad_total = jnp.sum(jnp.square(grad.astype(jnp.float32)))
    pre_total = jnp.sum(jnp.square(pre.astype(jnp.float32)))
    ratio = jnp.sqrt(grad_total / pre_total)
    scaled = (lax.optimization_barrier(pre).astype(jnp.float32) * ratio).astype(jnp.bfloat16)
    direction = scaled.reshape(N_TENSOR, NBR, NBC, BLOCK_ORDER, BLOCK_ORDER).transpose(1, 3, 0, 2, 4).reshape(D, COLS)
    left_out = left_state.at[tens, owner, slot].set(left_new)
    right_out = right_state.at[tens, owner, slot].set(right_new)
    return (direction, left_out, right_out)
```

```python
import functools

import jax
import jax.numpy as jnp
from jax import lax
from jax.experimental import pallas as pl
from jax.experimental.pallas import tpu as pltpu
from jax.sharding import PartitionSpec as P

N = 512
Q = 128
NZ, NY, NT = 8, 4, 8
SLOTS, NBLK, TOK = 2, 16, 256
BETA = 0.95
MESH = pl.DeviceIdType.MESH
RIGHT, LEFT = 0, 1
bf16, f32 = jnp.bfloat16, jnp.float32


def place():
    dp, t = lax.axis_index("dp"), lax.axis_index("tensor")
    return dp, t, dp // NY, lax.rem(dp, NY)


def ring(z, step):
    return lax.rem(z + step + NZ, NZ)


def remote(src, dst, send, recv, dp, t):
    return pltpu.make_async_remote_copy(
        src_ref=src, dst_ref=dst, send_sem=send, recv_sem=recv,
        device_id=(dp, t), device_id_type=MESH,
    )


def dot(a, b, ca, cb):
    return lax.dot_general(a, b, (((ca,), (cb,)), ((), ())), preferred_element_type=f32)


def barrier(peers):
    sem = pltpu.get_barrier_semaphore()
    for dp, t in peers:
        pl.semaphore_signal(sem, inc=1, device_id=(dp, t), device_id_type=MESH)
    pl.semaphore_wait(sem, len(peers))


def held(own_ref, slot_ref, device, slot):
    block, used = jnp.int32(0), jnp.int32(0)
    for b in range(NBLK):
        hit = (own_ref[b] == device) & (slot_ref[b] == slot)
        block = jnp.where(hit, b, block)
        used = jnp.where(hit, 1, used)
    return block, used


def chunk_of(z, k):
    far = 4 - (k + 1) // 2
    return ring(z, far if k % 2 else -far)


def grads_kernel(
    a_ref, o_ref, own_ref, slot_ref, h_ref,
    a_buf, ot_buf, snd, rcv, gath, stage,
    o_send, o_recv, own_sem, a_send, a_recv, f_send, f_recv,
    r_send, r_recv, g_send, g_recv, y_send, y_recv,
):
    dp, t, z, y = place()
    core = lax.rem(t, 2)
    twin = t + 1 - 2 * core
    ys = [lax.rem(y + j, NY) for j in range(NY)]
    ydp = [z * NY + yj for yj in ys]
    side = [ring(z, 1) * NY + y, ring(z, -1) * NY + y]
    barrier([(ydp[1], t), (ydp[2], t), (ydp[3], t), (side[0], t), (side[1], t), (dp, twin)])

    def columns(c, p, yj):
        return a_ref.at[:, pl.ds(pl.multiple_of((2 * c + p) * N + yj * Q, Q), Q)]

    def a_part(c, p, src):
        return a_buf.at[c, p, pl.ds(pl.multiple_of(src * TOK, TOK), TOK)]

    ot_buf[y] = o_ref[...].T
    waits = []

    def o_copy(j, src):
        return remote(ot_buf.at[src], ot_buf.at[src], o_send.at[j], o_recv.at[j], ydp[j], t)

    for j in (1, 3, 2):
        o_copy(j, y).start()

    def a_copy(k, j, src):
        c = chunk_of(z, k)
        return remote(
            columns(c, core, ys[j]), a_part(c, core, src),
            a_send.at[k, j], a_recv.at[k, j], ydp[j], t,
        )

    def own_copy(k, p):
        c = chunk_of(z, k)
        return pltpu.make_async_copy(columns(c, p, y), a_part(c, p, y), own_sem.at[k, p])

    for k in range(NZ):
        for j in (2, 1, 3):
            a_copy(k, j, y).start()
        for p in range(2):
            own_copy(k, p).start()

    def f_copy(k, j, p):
        part = a_part(chunk_of(z, k), p, ys[(NY - j) % NY])
        return remote(part, part, f_send.at[k, j], f_recv.at[k, j], dp, twin)

    def forward(k):
        for j in (1, 3, 2):
            a_copy(k, j, ys[(NY - j) % NY]).wait_recv()
            f_copy(k, j, core).start()

    def chain(d, s, p, to):
        return remote(snd.at[d, s, p], rcv.at[d, s, p], r_send.at[d, s, p], r_recv.at[d, s, p], to, t)

    forward(0)
    for j in (1, 3, 2):
        o_copy(j, ys[(NY - j) % NY]).wait_recv()
    sent = []
    for k in range(NZ):
        c = chunk_of(z, k)
        if k + 1 < NZ:
            forward(k + 1)
        for p in range(2):
            own_copy(k, p).wait()
        for j in (1, 3, 2):
            f_copy(k, j, 1 - core).wait_recv()
        acts = jnp.concatenate([a_buf[c, 0], a_buf[c, 1]], axis=1)
        outs = jnp.concatenate([ot_buf[j] for j in range(NY)], axis=1)
        part = dot(outs, acts, 1, 0)
        part = [part[:, :Q], part[:, Q:]]
        if k == 0:
            moves = [(RIGHT, 0, 0), (LEFT, 0, 1)]
        elif k < NZ - 1:
            moves = [((RIGHT if k % 2 else LEFT), (k + 1) // 2, p) for p in range(2)]
        else:
            moves = []
        for d, s, p in moves:
            value = part[p]
            if s > 1 or (s == 1 and p == d):
                chain(d, s - 1, p, side[d]).wait_recv()
                value = value + rcv[d, s - 1, p].astype(f32)
            snd[d, s, p] = value.astype(bf16)
            chain(d, s, p, side[d]).start()
            sent.append((d, s, p))
        if k == NZ - 1:
            for p in range(2):
                for d in (RIGHT, LEFT):
                    chain(d, 3, p, side[d]).wait_recv()
                total = part[p] + rcv[RIGHT, 3, p].astype(f32) + rcv[LEFT, 3, p].astype(f32)
                gath[2 * z + p] = total.astype(bf16)

    def g_copy(d, s, p):
        piece = gath.at[2 * ring(z, -s if d == RIGHT else s) + p]
        return remote(piece, piece, g_send.at[d, s, p], g_recv.at[d, s, p], side[d], t)

    def g_wait(d, s, p):
        piece = gath.at[2 * ring(z, -s - 1 if d == RIGHT else s + 1) + p]
        remote(piece, piece, g_send.at[d, s, p], g_recv.at[d, s, p], side[d], t).wait_recv()

    hops = [(s, p, d) for s in range(4) for p in range(2) for d in (RIGHT, LEFT) if s < 3 or p == d]
    for s, p, d in hops:
        if s > 0:
            g_wait(d, s - 1, p)
        g_copy(d, s, p).start()
    for d in (RIGHT, LEFT):
        g_wait(d, 2, 1 - d)
        g_wait(d, 3, d)

    def y_copy(j, src):
        return remote(stage.at[j], h_ref.at[src], y_send.at[j], y_recv.at[j], ydp[j], t)

    for j in (2, 1, 3, 0):
        for s in range(SLOTS):
            block, _ = held(own_ref, slot_ref, ydp[j], s)
            if j:
                stage[j, s] = gath[block]
            else:
                h_ref[y, s] = gath[block]
        if j:
            y_copy(j, y).start()
    for j in (1, 3, 2):
        y_copy(j, ys[(NY - j) % NY]).wait_recv()

    for j in (1, 2, 3):
        o_copy(j, y).wait_send()
        y_copy(j, y).wait_send()
        for k in range(NZ):
            a_copy(k, j, y).wait_send()
            f_copy(k, j, core).wait_send()
    for d, s, p in sent:
        chain(d, s, p, side[d]).wait_send()
    for s, p, d in hops:
        g_copy(d, s, p).wait_send()


def root(mat, eye):
    norm = jnp.sqrt(jnp.sum(mat * mat, axis=(0, 1), keepdims=True))
    scale = 2.5 / norm
    m = mat * scale
    mb = m.astype(bf16)
    square = dot(mb, mb, 1, 0)
    s2 = (1.5625 * eye - 0.625 * m + 0.0625 * square).astype(bf16)
    sm = (1.25 * m - 0.25 * square).astype(bf16)
    s4 = dot(s2, s2, 1, 0).astype(bf16)
    x = 1.5625 * eye - 0.3125 * m - 0.25 * dot(s4, sm, 1, 0)
    return (x * jnp.sqrt(jnp.sqrt(scale))).astype(bf16)


def update_kernel(used_ref, h_ref, l_ref, r_ref, lo_ref, ro_ref, p_ref, sum_ref):
    used = used_ref[pl.program_id(0)]

    @pl.when(used == 0)
    def _():
        lo_ref[...] = l_ref[...]
        ro_ref[...] = r_ref[...]
        p_ref[...] = jnp.zeros_like(p_ref)
        sum_ref[...] = jnp.zeros_like(sum_ref)

    @pl.when(used != 0)
    def _():
        h = jnp.concatenate([h_ref[j, 0] for j in range(NY)], axis=1)
        left = BETA * l_ref[0] + dot(h, h, 0, 0)
        lo_ref[0] = left
        right = BETA * r_ref[0] + dot(h, h, 1, 1)
        ro_ref[0] = right
        eye = (
            lax.broadcasted_iota(jnp.int32, (N, N), 0) == lax.broadcasted_iota(jnp.int32, (N, N), 1)
        ).astype(f32)
        part = dot(root(right, eye), h, 1, 0).astype(bf16)
        pre = dot(root(left, eye), part, 1, 1).astype(bf16)
        p_ref[0] = pre
        hf, pf = h.astype(f32), pre.astype(f32)
        sum_ref[0, 0] = jnp.broadcast_to(jnp.sum(hf * hf, axis=(0, 1), keepdims=True), (8, 128))
        sum_ref[0, 1] = jnp.broadcast_to(jnp.sum(pf * pf, axis=(0, 1), keepdims=True), (8, 128))


def back_kernel(
    p_ref, sum_ref, own_ref, slot_ref, out_ref,
    got, snd, rcv, mine, last, sums,
    y_send, y_recv, r_send, r_recv, l_send, l_recv, s_send, s_recv,
):
    dp, t, z, y = place()
    ys = [lax.rem(y + j, NY) for j in range(NY)]
    ydp = [z * NY + yj for yj in ys]
    side = [ring(z, 1) * NY + y, ring(z, -1) * NY + y]
    ts = [lax.rem(t + j, NT) for j in range(NT)]
    zdp = [ring(z, j) * NY + y for j in range(NZ)]
    barrier(
        [(ydp[j], t) for j in range(1, NY)]
        + [(dp, ts[j]) for j in range(1, NT)]
        + [(zdp[j], t) for j in range(1, NZ)]
    )

    def y_copy(j, src):
        rows = pl.ds(pl.multiple_of(ys[j] * Q, Q), Q)
        return remote(p_ref.at[:, rows], got.at[src], y_send.at[j], y_recv.at[j], ydp[j], t)

    for j in (2, 1, 3):
        y_copy(j, y).start()

    stages = [
        (NT, lambda j: (dp, ts[j])),
        (NY, lambda j: (ydp[j], t)),
        (NZ, lambda j: (zdp[j], t)),
    ]

    def s_copy(i, j):
        return remote(
            sums.at[i, 0], sums.at[i, j], s_send.at[i, j], s_recv.at[i, j], *stages[i][1](j)
        )

    def sum_start(i, value):
        sums[i, 0] = value
        for j in range(1, stages[i][0]):
            s_copy(i, j).start()

    def sum_end(i):
        for j in range(1, stages[i][0]):
            s_copy(i, j).wait_recv()
        return functools.reduce(jnp.add, [sums[i, j] for j in range(stages[i][0])])

    sum_start(0, sum_ref[0] + sum_ref[1])
    got[y] = p_ref[:, pl.ds(pl.multiple_of(y * Q, Q), Q)]
    sum_start(1, sum_end(0))
    for j in (1, 3, 2):
        y_copy(j, ys[(NY - j) % NY]).wait_recv()

    def chain(d, s, p, to):
        return remote(snd.at[d, s, p], rcv.at[d, s, p], r_send.at[d, s, p], r_recv.at[d, s, p], to, t)

    def place_of(c, p):
        b = 2 * c + p
        owner = own_ref[b]
        return owner // NY, lax.rem(owner, NY), slot_ref[b]

    sent = []
    for s in range(4):
        for p in range(2):
            for d in (RIGHT, LEFT):
                if s == 0 and p != d:
                    continue
                oz, oy, os = place_of(ring(z, 4 - s if d == RIGHT else s - 4), p)
                value = got[oy, os]
                if s > 1 or (s == 1 and p == d):
                    chain(d, s - 1, p, side[d]).wait_recv()
                    value = jnp.where(oz == z, value, rcv[d, s - 1, p])
                snd[d, s, p] = value
                chain(d, s, p, side[d]).start()
                sent.append((d, s, p))
        if s == 1:
            sum_start(2, sum_end(1))
    total = sum_end(2)
    ratio = jnp.sqrt(total[0] / total[1])[0:1, 0:1]
    for p in range(2):
        oz, oy, os = place_of(z, p)
        for d in (RIGHT, LEFT):
            chain(d, 3, p, side[d]).wait_recv()
        behind = ring(z, -oz)
        from_left = (behind < 4) | ((behind == 4) & (p == 0))
        value = jnp.where(from_left, rcv[RIGHT, 3, p], rcv[LEFT, 3, p])
        value = jnp.where(oz == z, got[oy, os], value)
        mine[p] = (value.astype(f32) * ratio).astype(bf16)

    def l_copy(p):
        return remote(
            mine.at[p], last.at[lax.rem(y, 2)], l_send.at[p], l_recv.at[lax.rem(y, 2)],
            z * NY + 2 * p + y // 2, t,
        )

    for p in range(2):
        to = 2 * p + y // 2

        @pl.when(to != y)
        def _():
            l_copy(p).start()

        @pl.when(to == y)
        def _():
            last[lax.rem(y, 2)] = mine[p]

    for q in range(2):
        src = 2 * lax.rem(y, 2) + q

        @pl.when(src != y)
        def _():
            remote(
                mine.at[0], last.at[q], l_send.at[0], l_recv.at[q], z * NY + src, t
            ).wait_recv()

        out_ref[pl.ds(q * Q, Q)] = last[q]

    for p in range(2):
        @pl.when(2 * p + y // 2 != y)
        def _():
            l_copy(p).wait_send()
    for j in range(1, NY):
        y_copy(j, y).wait_send()
    for i in range(3):
        for j in range(1, stages[i][0]):
            s_copy(i, j).wait_send()
    for d, s, p in sent:
        chain(d, s, p, side[d]).wait_send()


VMEM = pl.BlockSpec(memory_space=pltpu.VMEM)
SMEM = pl.BlockSpec(memory_space=pltpu.SMEM)
ANY = pl.BlockSpec(memory_space=pl.ANY)
DMA = pltpu.SemaphoreType.DMA


def shards(activations, out_grads, owner, slot, left_state, right_state):
    own, where = owner[0], slot[0]
    h = pl.pallas_call(
        grads_kernel,
        out_shape=jax.ShapeDtypeStruct((NY, SLOTS, N, Q), bf16),
        in_specs=[ANY, VMEM, SMEM, SMEM],
        out_specs=VMEM,
        scratch_shapes=[
            pltpu.VMEM((NZ, 2, NY * TOK, Q), bf16),
            pltpu.VMEM((NY, N, TOK), bf16),
            pltpu.VMEM((2, 4, 2, N, Q), bf16),
            pltpu.VMEM((2, 4, 2, N, Q), bf16),
            pltpu.VMEM((NBLK, N, Q), bf16),
            pltpu.VMEM((NY, SLOTS, N, Q), bf16),
            DMA((NY,)), DMA((NY,)), DMA((NZ, 2)), DMA((NZ, NY)), DMA((NZ, NY)),
            DMA((NZ, NY)), DMA((NZ, NY)), DMA((2, 4, 2)), DMA((2, 4, 2)),
            DMA((2, 4, 2)), DMA((2, 4, 2)), DMA((NY,)), DMA((NY,)),
        ],
        compiler_params=pltpu.CompilerParams(
            collective_id=0, has_side_effects=True, vmem_limit_bytes=40 * 2**20
        ),
        name="grads",
    )(activations, out_grads, own, where)

    me = lax.axis_index("dp")
    used = jnp.any(
        (own[None] == me) & (where[None] == jnp.arange(SLOTS, dtype=jnp.int32)[:, None]), axis=1
    ).astype(jnp.int32)
    state = pl.BlockSpec((1, N, N), lambda s: (s, 0, 0))
    left_out, right_out, pre, sums = pl.pallas_call(
        update_kernel,
        grid=(SLOTS,),
        out_shape=[
            jax.ShapeDtypeStruct((SLOTS, N, N), f32),
            jax.ShapeDtypeStruct((SLOTS, N, N), f32),
            jax.ShapeDtypeStruct((SLOTS, N, N), bf16),
            jax.ShapeDtypeStruct((SLOTS, 2, 8, 128), f32),
        ],
        in_specs=[SMEM, pl.BlockSpec((NY, 1, N, Q), lambda s: (0, s, 0, 0)), state, state],
        out_specs=[state, state, state, pl.BlockSpec((1, 2, 8, 128), lambda s: (s, 0, 0, 0))],
        compiler_params=pltpu.CompilerParams(vmem_limit_bytes=40 * 2**20),
        name="update",
    )(used, h, left_state[0, 0], right_state[0, 0])

    direction = pl.pallas_call(
        back_kernel,
        out_shape=jax.ShapeDtypeStruct((TOK, N), bf16),
        in_specs=[VMEM, VMEM, SMEM, SMEM],
        out_specs=VMEM,
        scratch_shapes=[
            pltpu.VMEM((NY, SLOTS, Q, N), bf16),
            pltpu.VMEM((2, 4, 2, Q, N), bf16),
            pltpu.VMEM((2, 4, 2, Q, N), bf16),
            pltpu.VMEM((2, Q, N), bf16),
            pltpu.VMEM((2, Q, N), bf16),
            pltpu.VMEM((3, NT, 2, 8, 128), f32),
            DMA((NY,)), DMA((NY,)), DMA((2, 4, 2)), DMA((2, 4, 2)),
            DMA((2,)), DMA((2,)), DMA((3, NT)), DMA((3, NT)),
        ],
        compiler_params=pltpu.CompilerParams(
            collective_id=1, has_side_effects=True, vmem_limit_bytes=40 * 2**20
        ),
        name="back",
    )(pre, sums, own, where)
    return direction, left_out[None, None], right_out[None, None]


def solution(mesh):
    return jax.shard_map(
        shards,
        mesh=mesh,
        in_specs=(
            P("dp", None),
            P("dp", "tensor"),
            P("tensor", None),
            P("tensor", None),
            P("tensor", "dp", None, None, None),
            P("tensor", "dp", None, None, None),
        ),
        out_specs=(
            P("dp", "tensor"),
            P("tensor", "dp", None, None, None),
            P("tensor", "dp", None, None, None),
        ),
        check_vma=False,
    )
```

```python
import functools

import jax
import jax.numpy as jnp
from jax import lax
from jax.experimental import pallas as pl
from jax.experimental.pallas import tpu as pltpu
from jax.sharding import PartitionSpec as P

N = 512
Q = 128
NZ, NY, NX, NT = 8, 4, 4, 8
SLOTS, NBLK, TOK = 2, 16, 256
XTOK = TOK // NX
EXTRA = 16
BETA = 0.95
MESH = pl.DeviceIdType.MESH
RIGHT, LEFT = 0, 1
bf16, f32 = jnp.bfloat16, jnp.float32


def place():
    dp, t = lax.axis_index("dp"), lax.axis_index("tensor")
    return dp, t, dp // NY, lax.rem(dp, NY)


def ring(z, step):
    return lax.rem(z + step + NZ, NZ)


def remote(src, dst, send, recv, dp, t):
    return pltpu.make_async_remote_copy(
        src_ref=src, dst_ref=dst, send_sem=send, recv_sem=recv,
        device_id=(dp, t), device_id_type=MESH,
    )


def dot(a, b, ca, cb):
    return lax.dot_general(a, b, (((ca,), (cb,)), ((), ())), preferred_element_type=f32)


def held(own_ref, slot_ref, device, slot):
    block, used = jnp.int32(0), jnp.int32(0)
    for b in range(NBLK):
        hit = (own_ref[0, b] == device) & (slot_ref[0, b] == slot)
        block = jnp.where(hit, b, block)
        used = jnp.where(hit, 1, used)
    return block, used


def chunk_of(z, k):
    far = 4 - (k + 1) // 2
    return ring(z, far if k % 2 else -far)


def moves_of(k):
    if k == 0:
        return [(RIGHT, 0, 0), (LEFT, 0, 1)]
    if k == NZ - 1:
        return []
    return [((RIGHT if k % 2 else LEFT), (k + 1) // 2, p) for p in range(2)]


def step_kernel(
    a_ref, o_ref, own_ref, slot_ref, l_ref, r_ref, out_ref, lo_ref, ro_ref,
    l_buf, r_buf, tp, got, t_snd, t_rcv, t_fin, t_all,
    a_buf, o_buf, ot_buf, snd, rcv, gath, g_all, stage, h_buf, xl_buf, pre_buf, sums,
    st_sem, out_sem, t_send, t_recv, c_send, c_recv, ta_send, ta_recv,
    o_send, o_recv, own_sem, a_send, a_recv, x_send, x_recv, f_send, f_recv,
    r_send, r_recv, g_send, g_recv, ga_send, ga_recv, y_send, y_recv, s_send, s_recv,
):
    dp, t, z, y = place()
    core, x = lax.rem(t, 2), t // 2
    twin = t + 1 - 2 * core
    xs = [lax.rem(x + i, NX) for i in range(NX)]
    xt = [2 * xi + core for xi in xs]
    ys = [lax.rem(y + j, NY) for j in range(NY)]
    ydp = [z * NY + yj for yj in ys]
    side = [ring(z, 1) * NY + y, ring(z, -1) * NY + y]
    ts = [lax.rem(t + j, NT) for j in range(NT)]
    zdp = [ring(z, j) * NY + y for j in range(NZ)]

    def behind(j):
        return ys[(NY - j) % NY]

    def columns(c, p, yj):
        return pl.ds(pl.multiple_of((2 * c + p) * N + yj * Q, Q), Q)

    state_in = [
        pltpu.make_async_copy(ref.at[s], buf.at[s], st_sem.at[i, s])
        for s in range(SLOTS)
        for i, (ref, buf) in enumerate(((l_ref, l_buf), (r_ref, r_buf)))
    ]
    for copy in state_in:
        copy.start()
    peers = (
        [(ydp[j], t) for j in range(1, NY)]
        + [(dp, ts[j]) for j in range(1, NT)]
        + [(zdp[j], t) for j in range(1, NZ)]
    )
    met = pltpu.get_barrier_semaphore()
    for peer in peers:
        pl.semaphore_signal(met, inc=1, device_id=peer, device_id_type=MESH)

    def own_copy(k, p):
        c = chunk_of(z, k)
        return pltpu.make_async_copy(
            a_ref.at[:, :, columns(c, p, y)], a_buf.at[c, p, :, 0], own_sem.at[k, p]
        )

    for k in range(NZ):
        for p in range(2):
            own_copy(k, p).start()
    o_buf[:, 0] = o_ref[...]

    row = lax.broadcasted_iota(jnp.int32, (N, N), 0)
    col = lax.broadcasted_iota(jnp.int32, (N, N), 1)
    eye = (row == col).astype(f32)

    for s in range(SLOTS):
        for copy in state_in[2 * s : 2 * s + 2]:
            copy.wait()
        both = jnp.where(row <= col, l_buf[s], r_buf[s]).astype(bf16)
        diag = jnp.sum(r_buf[s] * eye, axis=0, keepdims=True)
        diag = jnp.broadcast_to(diag, (EXTRA, N)).astype(bf16)
        for q in range(NY):
            tp[q, s, pl.ds(0, N)] = both[:, q * Q : (q + 1) * Q]
            tp[q, s, pl.ds(N, EXTRA)] = diag[:, q * Q : (q + 1) * Q]
    pl.semaphore_wait(met, len(peers))

    def t_copy(j, src):
        return remote(tp.at[ys[j]], got.at[src], t_send.at[j], t_recv.at[j], ydp[j], t)

    for j in (2, 1, 3):
        t_copy(j, y).start()
    got[y] = tp[y]

    def o_copy(j):
        return remote(o_ref, o_buf.at[:, j], o_send.at[j], o_recv.at[j], ydp[j], t)

    def a_copy(k, j):
        c = chunk_of(z, k)
        return remote(
            a_ref.at[x, :, columns(c, core, ys[j])], a_buf.at[c, core, x, j],
            a_send.at[k, j], a_recv.at[k, j], ydp[j], t,
        )

    for k in range(NZ):
        for j in (2, 1, 3):
            a_copy(k, j).start()
    for j in (2, 1, 3):
        o_copy(j).start()

    def x_copy(k, i, src):
        part = a_buf.at[chunk_of(z, k), core, src, 1:]
        return remote(part, part, x_send.at[k, i], x_recv.at[k, i], dp, xt[i])

    def f_copy(k, p):
        part = a_buf.at[chunk_of(z, k), p, :, 1:]
        return remote(part, part, f_send.at[k], f_recv.at[k], dp, twin)

    def along_x(k):
        for j in (1, 3, 2):
            a_copy(k, j).wait_recv()
        for i in (2, 1, 3):
            x_copy(k, i, x).start()

    def to_twin(k):
        for i in (1, 3, 2):
            x_copy(k, i, xs[NX - i]).wait_recv()
        f_copy(k, core).start()

    def t_chain(d, s, p):
        return remote(
            t_snd.at[d, s, p], t_rcv.at[d, s, p], c_send.at[d, s, p], c_recv.at[d, s, p], side[d], t
        )

    def place_of(c, p):
        owner = own_ref[0, 2 * c + p]
        return owner // NY, lax.rem(owner, NY), slot_ref[0, 2 * c + p]

    for j in (1, 3, 2):
        t_copy(j, behind(j)).wait_recv()
    for k in range(NZ):
        for d, s, p in moves_of(k):
            oz, oy, os = place_of(chunk_of(z, k), p)
            value = got[oy, os]
            if s > 1 or (s == 1 and p == d):
                t_chain(d, s - 1, p).wait_recv()
                value = jnp.where(oz == z, value, t_rcv[d, s - 1, p])
            t_snd[d, s, p] = value
            t_chain(d, s, p).start()
        along_x(k)
        if k >= 1:
            to_twin(k - 1)
    for p in range(2):
        oz, oy, os = place_of(z, p)
        for d in (RIGHT, LEFT):
            t_chain(d, 3, p).wait_recv()
        back = ring(z, -oz)
        from_left = (back < 4) | ((back == 4) & (p == 0))
        value = jnp.where(from_left, t_rcv[RIGHT, 3, p], t_rcv[LEFT, 3, p])
        t_fin[p] = jnp.where(oz == z, got[oy, os], value)
    to_twin(NZ - 1)

    def ta_copy(j, src):
        return remote(t_fin.at[ys[j] // 2], t_all.at[src], ta_send.at[j], ta_recv.at[j], ydp[j], t)

    def ga_copy(j, src):
        piece = gath.at[2 * z + ys[j] // 2]
        return remote(piece, g_all.at[src], ga_send.at[j], ga_recv.at[j], ydp[j], t)

    for j in (2, 1, 3):
        ta_copy(j, y).start()
    t_all[y] = t_fin[y // 2]

    def chain(d, s, p):
        return remote(
            snd.at[d, s, p], rcv.at[d, s, p], r_send.at[d, s, p], r_recv.at[d, s, p], side[d], t
        )

    for j in (1, 3, 2):
        o_copy(j).wait_recv()
    ot_buf[...] = o_buf[...].reshape(NY * TOK, N).T
    for k in range(NZ):
        c = chunk_of(z, k)
        for p in range(2):
            own_copy(k, p).wait()
        f_copy(k, 1 - core).wait_recv()
        acts = jnp.concatenate([a_buf[c, p].reshape(NY * TOK, Q) for p in range(2)], axis=1)
        part = dot(ot_buf[...], acts, 1, 0)
        part = [part[:, :Q], part[:, Q:]]
        for d, s, p in moves_of(k):
            value = part[p]
            if s > 1 or (s == 1 and p == d):
                chain(d, s - 1, p).wait_recv()
                value = value + rcv[d, s - 1, p].astype(f32)
            snd[d, s, p] = value.astype(bf16)
            chain(d, s, p).start()
    gsum = jnp.zeros((1, 1), f32)
    for p in range(2):
        for d in (RIGHT, LEFT):
            chain(d, 3, p).wait_recv()
        total = part[p] + rcv[RIGHT, 3, p].astype(f32) + rcv[LEFT, 3, p].astype(f32)
        total = total.astype(bf16)
        gath[2 * z + p] = total
        total = total.astype(f32)
        gsum = gsum + jnp.sum(total * total, axis=(0, 1), keepdims=True)

    def g_copy(d, s, p):
        piece = gath.at[2 * ring(z, -s if d == RIGHT else s) + p]
        return remote(piece, piece, g_send.at[d, s, p], g_recv.at[d, s, p], side[d], t)

    def g_wait(d, s, p):
        piece = gath.at[2 * ring(z, -s - 1 if d == RIGHT else s + 1) + p]
        remote(piece, piece, g_send.at[d, s, p], g_recv.at[d, s, p], side[d], t).wait_recv()

    def hop(s):
        for p in range(2):
            for d in (RIGHT, LEFT):
                if s < 3 or p == d:
                    if s > 0:
                        g_wait(d, s - 1, p)
                    g_copy(d, s, p).start()

    hop(0)
    for j in (2, 1, 3):
        ga_copy(j, y).start()
    g_all[y] = gath[2 * z + y // 2]

    for j in (1, 3, 2):
        ta_copy(j, behind(j)).wait_recv()
    both = jnp.concatenate([t_all[q, pl.ds(0, N)] for q in range(NY)], axis=1)
    diag = jnp.concatenate([t_all[q, pl.ds(N, EXTRA)] for q in range(NY)], axis=1)[0:1]
    flip = both.T.astype(f32)
    both = both.astype(f32)
    l_old = jnp.where(row <= col, both, flip)
    r_old = jnp.where(row > col, both, flip)
    r_old = jnp.where(row == col, diag.astype(f32), r_old)
    for j in (1, 3, 2):
        ga_copy(j, behind(j)).wait_recv()
    hop(1)
    h = jnp.concatenate([g_all[q] for q in range(NY)], axis=1)
    xr = root(BETA * r_old + dot(h, h, 1, 1), eye)
    part = dot(xr, h, 1, 0).astype(bf16)
    xl_buf[...] = root(BETA * l_old + dot(h, h, 0, 0), eye)
    half = xl_buf[pl.ds(pl.multiple_of(lax.rem(y, 2) * TOK, TOK), TOK)]
    pre = dot(half, part, 1, 1).astype(bf16)
    pre_buf[...] = pre
    pf = pre.astype(f32)
    psum = jnp.sum(pf * pf, axis=(0, 1), keepdims=True)

    stages = [
        (NT, lambda j: (dp, ts[j])),
        (NY, lambda j: (ydp[j], t)),
        (NZ, lambda j: (zdp[j], t)),
    ]

    def s_copy(i, j):
        return remote(
            sums.at[i, 0], sums.at[i, j], s_send.at[i, j], s_recv.at[i, j], *stages[i][1](j)
        )

    def sum_start(i, value):
        sums[i, 0] = value
        for j in range(1, stages[i][0]):
            s_copy(i, j).start()

    def sum_end(i):
        for j in range(1, stages[i][0]):
            s_copy(i, j).wait_recv()
        return functools.reduce(jnp.add, [sums[i, j] for j in range(stages[i][0])])

    sum_start(0, jnp.stack([jnp.broadcast_to(v, (8, 128)) for v in (gsum, psum)]))
    hop(2)
    sum_start(1, sum_end(0))
    sum_start(2, sum_end(1))
    hop(3)
    total = sum_end(2)
    ratio = jnp.sqrt(total[0] / total[1])[0:1, 0:1]
    out_ref[...] = (pre_buf[...].astype(f32) * ratio).astype(bf16)

    def y_copy(j, src):
        return remote(stage.at[j], h_buf.at[src], y_send.at[j], y_recv.at[j], ydp[j], t)

    picks = [[held(own_ref, slot_ref, ydp[j], s) for s in range(SLOTS)] for j in range(NY)]
    for d in (RIGHT, LEFT):
        g_wait(d, 2, 1 - d)
        g_wait(d, 3, d)
    for j in (2, 1, 3, 0):
        for s in range(SLOTS):
            if j:
                stage[j, s] = gath[picks[j][s][0]]
            else:
                h_buf[y, s] = gath[picks[j][s][0]]
        if j:
            y_copy(j, y).start()
    for j in (1, 3, 2):
        y_copy(j, behind(j)).wait_recv()
    state_out = []
    for s in range(SLOTS):
        used = picks[0][s][1] != 0
        h = jnp.concatenate([h_buf[q, s] for q in range(NY)], axis=1)
        for i, (ref, buf, axis) in enumerate(((lo_ref, l_buf, 0), (ro_ref, r_buf, 1))):
            old = buf[s]
            buf[s] = jnp.where(used, BETA * old + dot(h, h, axis, axis), old)
            state_out.append(pltpu.make_async_copy(buf.at[s], ref.at[s], out_sem.at[i, s]))
            state_out[-1].start()

    for j in (1, 2, 3):
        t_copy(j, y).wait_send()
        o_copy(j).wait_send()
        ta_copy(j, y).wait_send()
        ga_copy(j, y).wait_send()
        y_copy(j, y).wait_send()
    for k in range(NZ):
        f_copy(k, core).wait_send()
        for j in (1, 2, 3):
            a_copy(k, j).wait_send()
            x_copy(k, j, x).wait_send()
        for d, s, p in moves_of(k):
            t_chain(d, s, p).wait_send()
            chain(d, s, p).wait_send()
            if s < 3 or p == d:
                g_copy(d, s, p).wait_send()
    for d in (RIGHT, LEFT):
        g_copy(d, 0, 1 - d).wait_send()
    for i in range(3):
        for j in range(1, stages[i][0]):
            s_copy(i, j).wait_send()
    for copy in state_out:
        copy.wait()


def root(mat, eye):
    norm = jnp.sqrt(jnp.sum(mat * mat, axis=(0, 1), keepdims=True))
    scale = 2.5 / norm
    m = mat * scale
    mb = m.astype(bf16)
    square = dot(mb, mb, 1, 0)
    s2 = (1.5625 * eye - 0.625 * m + 0.0625 * square).astype(bf16)
    sm = (1.25 * m - 0.25 * square).astype(bf16)
    s4 = dot(s2, s2, 1, 0).astype(bf16)
    x = 1.5625 * eye - 0.3125 * m - 0.25 * dot(s4, sm, 1, 0)
    return (x * jnp.sqrt(jnp.sqrt(scale))).astype(bf16)


VMEM = pl.BlockSpec(memory_space=pltpu.VMEM)
SMEM = pl.BlockSpec(memory_space=pltpu.SMEM)
HBM = pl.BlockSpec(memory_space=pltpu.MemorySpace.HBM)
DMA = pltpu.SemaphoreType.DMA


def shards(activations, out_grads, owner, slot, left_state, right_state):
    direction, left_out, right_out = pl.pallas_call(
        step_kernel,
        out_shape=[
            jax.ShapeDtypeStruct((TOK, N), bf16),
            jax.ShapeDtypeStruct((SLOTS, N, N), f32),
            jax.ShapeDtypeStruct((SLOTS, N, N), f32),
        ],
        in_specs=[HBM, VMEM, SMEM, SMEM, HBM, HBM],
        out_specs=[VMEM, HBM, HBM],
        scratch_shapes=[
            pltpu.VMEM((SLOTS, N, N), f32),
            pltpu.VMEM((SLOTS, N, N), f32),
            pltpu.VMEM((NY, SLOTS, N + EXTRA, Q), bf16),
            pltpu.VMEM((NY, SLOTS, N + EXTRA, Q), bf16),
            pltpu.VMEM((2, 4, 2, N + EXTRA, Q), bf16),
            pltpu.VMEM((2, 4, 2, N + EXTRA, Q), bf16),
            pltpu.VMEM((2, N + EXTRA, Q), bf16),
            pltpu.VMEM((NY, N + EXTRA, Q), bf16),
            pltpu.VMEM((NZ, 2, NX, NY, XTOK, Q), bf16),
            pltpu.VMEM((NX, NY, XTOK, N), bf16),
            pltpu.VMEM((N, NY * TOK), bf16),
            pltpu.VMEM((2, 4, 2, N, Q), bf16),
            pltpu.VMEM((2, 4, 2, N, Q), bf16),
            pltpu.VMEM((NBLK, N, Q), bf16),
            pltpu.VMEM((NY, N, Q), bf16),
            pltpu.VMEM((NY, SLOTS, N, Q), bf16),
            pltpu.VMEM((NY, SLOTS, N, Q), bf16),
            pltpu.VMEM((N, N), bf16),
            pltpu.VMEM((TOK, N), bf16),
            pltpu.VMEM((3, NT, 2, 8, 128), f32),
            DMA((2, SLOTS)), DMA((2, SLOTS)),
            DMA((NY,)), DMA((NY,)),
            DMA((2, 4, 2)), DMA((2, 4, 2)),
            DMA((NY,)), DMA((NY,)),
            DMA((NY,)), DMA((NY,)),
            DMA((NZ, 2)),
            DMA((NZ, NY)), DMA((NZ, NY)),
            DMA((NZ, NX)), DMA((NZ, NX)),
            DMA((NZ,)), DMA((NZ,)),
            DMA((2, 4, 2)), DMA((2, 4, 2)),
            DMA((2, 4, 2)), DMA((2, 4, 2)),
            DMA((NY,)), DMA((NY,)),
            DMA((NY,)), DMA((NY,)),
            DMA((3, NT)), DMA((3, NT)),
        ],
        compiler_params=pltpu.CompilerParams(
            collective_id=0, has_side_effects=True, vmem_limit_bytes=56 * 2**20
        ),
        name="step",
    )(
        activations.reshape(NX, XTOK, -1), out_grads.reshape(NX, XTOK, N), owner, slot,
        left_state[0, 0], right_state[0, 0],
    )
    return direction, left_out[None, None], right_out[None, None]


def solution(mesh):
    return jax.shard_map(
        shards,
        mesh=mesh,
        in_specs=(
            P("dp", None),
            P("dp", "tensor"),
            P("tensor", None),
            P("tensor", None),
            P("tensor", "dp", None, None, None),
            P("tensor", "dp", None, None, None),
        ),
        out_specs=(
            P("dp", "tensor"),
            P("tensor", "dp", None, None, None),
            P("tensor", "dp", None, None, None),
        ),
        check_vma=False,
    )
```

```python
import functools

import jax
import jax.numpy as jnp
from jax import lax
from jax.experimental import pallas as pl
from jax.experimental.pallas import tpu as pltpu
from jax.sharding import PartitionSpec as P

N = 512
HALF = 256
Q = 128
NZ, NY, NT = 8, 4, 8
SLOTS, NBLK, TOK = 2, 16, 256
EXTRA = 16
BETA = 0.95
MESH = pl.DeviceIdType.MESH
RIGHT, LEFT = 0, 1
bf16, f32 = jnp.bfloat16, jnp.float32


def place():
    dp, t = lax.axis_index("dp"), lax.axis_index("tensor")
    return dp, t, dp // NY, lax.rem(dp, NY)


def ring(z, step):
    return lax.rem(z + step + NZ, NZ)


def remote(src, dst, send, recv, dp, t):
    return pltpu.make_async_remote_copy(
        src_ref=src, dst_ref=dst, send_sem=send, recv_sem=recv,
        device_id=(dp, t), device_id_type=MESH,
    )


def dot(a, b, ca, cb):
    return lax.dot_general(a, b, (((ca,), (cb,)), ((), ())), preferred_element_type=f32)


def held(own_ref, slot_ref, device, slot):
    block, used = jnp.int32(0), jnp.int32(0)
    for b in range(NBLK):
        hit = (own_ref[0, b] == device) & (slot_ref[0, b] == slot)
        block = jnp.where(hit, b, block)
        used = jnp.where(hit, 1, used)
    return block, used


def chunk_of(z, k):
    far = 4 - (k + 1) // 2
    return ring(z, far if k % 2 else -far)


def moves_of(k):
    if k == 0:
        return [(RIGHT, 0, 0), (LEFT, 0, 1)]
    if k == NZ - 1:
        return []
    return [((RIGHT if k % 2 else LEFT), (k + 1) // 2, p) for p in range(2)]


def step_kernel(
    a_ref, o_ref, own_ref, slot_ref, l_ref, r_ref, out_ref, h_ref,
    l_buf, r_buf, tp, got, t_snd, t_rcv, t_fin, t_all,
    a_buf, ot_buf, snd, rcv, gath_0, gath_1, g_all, stage, xl_buf, pre_buf, sums,
    st_sem, t_send, t_recv, c_send, c_recv, ta_send, ta_recv,
    o_send, o_recv, own_sem, a_send, a_recv, f_send, f_recv,
    r_send, r_recv, g_send, g_recv, ga_send, ga_recv, y_send, y_recv, s_send, s_recv,
):
    dp, t, z, y = place()
    core = lax.rem(t, 2)
    gath = (gath_0, gath_1)
    twin = t + 1 - 2 * core
    ys = [lax.rem(y + j, NY) for j in range(NY)]
    ydp = [z * NY + yj for yj in ys]
    side = [ring(z, 1) * NY + y, ring(z, -1) * NY + y]
    ts = [lax.rem(t + j, NT) for j in range(NT)]
    zdp = [ring(z, j) * NY + y for j in range(NZ)]

    def behind(j):
        return ys[(NY - j) % NY]

    def columns(c, p, yj):
        return pl.ds(pl.multiple_of((2 * c + p) * N + yj * Q, Q), Q)

    state_in = [
        pltpu.make_async_copy(ref.at[s], buf.at[s], st_sem.at[i, s])
        for s in range(SLOTS)
        for i, (ref, buf) in enumerate(((l_ref, l_buf), (r_ref, r_buf)))
    ]
    for copy in state_in:
        copy.start()
    peers = (
        [(ydp[j], t) for j in range(1, NY)]
        + [(dp, ts[j]) for j in range(1, NT)]
        + [(zdp[j], t) for j in range(1, NZ)]
    )
    met = pltpu.get_barrier_semaphore()
    for peer in peers:
        pl.semaphore_signal(met, inc=1, device_id=peer, device_id_type=MESH)

    def own_copy(k, p):
        c = chunk_of(z, k)
        return pltpu.make_async_copy(
            a_ref.at[:, columns(c, p, y)], a_buf.at[c, p, 0], own_sem.at[k, p]
        )

    for k in range(NZ):
        for p in range(2):
            own_copy(k, p).start()
    ot_buf[0] = o_ref[...].T

    row = lax.broadcasted_iota(jnp.int32, (N, N), 0)
    col = lax.broadcasted_iota(jnp.int32, (N, N), 1)
    def t_copy(j, s, src):
        return remote(
            tp.at[ys[j], s], got.at[src, s], t_send.at[j, s], t_recv.at[j, s], ydp[j], t
        )

    for s in range(SLOTS):
        for copy in state_in[2 * s : 2 * s + 2]:
            copy.wait()
        both = jnp.where(row <= col, l_buf[s], r_buf[s]).astype(bf16)
        diag = jnp.sum(jnp.where(row == col, r_buf[s], 0.0), axis=0, keepdims=True)
        diag = jnp.broadcast_to(diag, (EXTRA, N)).astype(bf16)
        for q in range(NY):
            tp[q, s, pl.ds(0, N)] = both[:, q * Q : (q + 1) * Q]
            tp[q, s, pl.ds(N, EXTRA)] = diag[:, q * Q : (q + 1) * Q]
        if s == 0:
            pl.semaphore_wait(met, len(peers))
        for j in (2, 1, 3):
            t_copy(j, s, y).start()

    def o_copy(j):
        return remote(ot_buf.at[0], ot_buf.at[j], o_send.at[j], o_recv.at[j], ydp[j], t)

    def a_copy(k, j):
        c = chunk_of(z, k)
        return remote(
            a_ref.at[:, columns(c, core, ys[j])], a_buf.at[c, core, j],
            a_send.at[k, j], a_recv.at[k, j], ydp[j], t,
        )

    def f_copy(k, p):
        part = a_buf.at[chunk_of(z, k), p, 1:]
        return remote(part, part, f_send.at[k], f_recv.at[k], dp, twin)

    def to_twin(k):
        for j in (1, 3, 2):
            a_copy(k, j).wait_recv()
        f_copy(k, core).start()

    for j in (2, 1, 3):
        o_copy(j).start()
    for k in range(NZ):
        for j in (2, 1, 3):
            a_copy(k, j).start()
    got[y] = tp[y]

    def t_chain(d, s, p):
        return remote(
            t_snd.at[d, s, p], t_rcv.at[d, s, p], c_send.at[d, s, p], c_recv.at[d, s, p], side[d], t
        )

    def place_of(c, p):
        owner = own_ref[0, 2 * c + p]
        return owner // NY, lax.rem(owner, NY), slot_ref[0, 2 * c + p]

    for s in range(SLOTS):
        for j in (1, 3, 2):
            t_copy(j, s, behind(j)).wait_recv()
    for k in range(NZ):
        for d, s, p in moves_of(k):
            oz, oy, os = place_of(chunk_of(z, k), p)
            value = got[oy, os]
            if s > 1 or (s == 1 and p == d):
                t_chain(d, s - 1, p).wait_recv()
                value = jnp.where(oz == z, value, t_rcv[d, s - 1, p])
            t_snd[d, s, p] = value
            t_chain(d, s, p).start()
    for p in range(2):
        oz, oy, os = place_of(z, p)
        for d in (RIGHT, LEFT):
            t_chain(d, 3, p).wait_recv()
        back = ring(z, -oz)
        from_left = (back < 4) | ((back == 4) & (p == 0))
        value = jnp.where(from_left, t_rcv[RIGHT, 3, p], t_rcv[LEFT, 3, p])
        t_fin[p] = jnp.where(oz == z, got[oy, os], value)

    def ta_copy(j, src):
        return remote(t_fin.at[ys[j] // 2], t_all.at[src], ta_send.at[j], ta_recv.at[j], ydp[j], t)

    def ga_copy(j, src, i):
        piece = gath[i].at[2 * z + ys[j] // 2]
        return remote(piece, g_all.at[src, i], ga_send.at[j, i], ga_recv.at[j, i], ydp[j], t)

    for j in (2, 1, 3):
        ta_copy(j, y).start()
    t_all[y] = t_fin[y // 2]

    def chain(d, s, p):
        return remote(
            snd.at[d, s, p], rcv.at[d, s, p], r_send.at[d, s, p], r_recv.at[d, s, p], side[d], t
        )

    for j in (1, 3, 2):
        o_copy(j).wait_recv()
    outs = jnp.concatenate([ot_buf[j] for j in range(NY)], axis=1)
    to_twin(0)
    for k in range(NZ):
        c = chunk_of(z, k)
        if k + 1 < NZ:
            to_twin(k + 1)
        for p in range(2):
            own_copy(k, p).wait()
        f_copy(k, 1 - core).wait_recv()
        acts = jnp.concatenate([a_buf[c, p].reshape(NY * TOK, Q) for p in range(2)], axis=1)
        part = dot(outs, acts, 1, 0)
        part = [part[:, :Q], part[:, Q:]]
        for d, s, p in moves_of(k):
            value = part[p]
            if s > 1 or (s == 1 and p == d):
                chain(d, s - 1, p).wait_recv()
                value = value + rcv[d, s - 1, p].astype(f32)
            snd[d, s, p] = value.astype(bf16)
            chain(d, s, p).start()
    gsum = jnp.zeros((1, 1), f32)
    for p in range(2):
        for d in (RIGHT, LEFT):
            chain(d, 3, p).wait_recv()
        total = part[p] + rcv[RIGHT, 3, p].astype(f32) + rcv[LEFT, 3, p].astype(f32)
        total = total.astype(bf16)
        for i in range(2):
            gath[i][2 * z + p] = total[i * HALF : (i + 1) * HALF]
        total = total.astype(f32)
        gsum = gsum + jnp.sum(total * total, axis=(0, 1), keepdims=True)

    def g_copy(d, s, p, i):
        piece = gath[i].at[2 * ring(z, -s if d == RIGHT else s) + p]
        return remote(piece, piece, g_send.at[d, s, p, i], g_recv.at[d, s, p, i], side[d], t)

    def g_wait(d, s, p, i):
        piece = gath[i].at[2 * ring(z, -s - 1 if d == RIGHT else s + 1) + p]
        remote(
            piece, piece, g_send.at[d, s, p, i], g_recv.at[d, s, p, i], side[d], t
        ).wait_recv()

    def hop(s, i):
        for p in range(2):
            for d in (RIGHT, LEFT):
                if s < 3 or p == d:
                    if s > 0:
                        g_wait(d, s - 1, p, i)
                    g_copy(d, s, p, i).start()

    def y_copy(j, src, i):
        return remote(
            stage.at[i, j], h_ref.at[i, src], y_send.at[i, j], y_recv.at[i, j], ydp[j], t
        )

    picks = [[held(own_ref, slot_ref, ydp[j], s)[0] for s in range(SLOTS)] for j in range(NY)]

    def to_owners(i):
        for d in (RIGHT, LEFT):
            g_wait(d, 2, 1 - d, i)
            g_wait(d, 3, d, i)
        for j in (2, 1, 3, 0):
            for s in range(SLOTS):
                if j:
                    stage[i, j, s] = gath[i][picks[j][s]]
                else:
                    h_ref[i, y, s] = gath[i][picks[j][s]]
            if j:
                y_copy(j, y, i).start()

    hop(0, 0)
    hop(0, 1)
    for j in (2, 1, 3):
        for i in range(2):
            ga_copy(j, y, i).start()
    for i in range(2):
        g_all[y, i] = gath[i][2 * z + y // 2]

    eye = (row == col).astype(f32)
    for j in (1, 3, 2):
        ta_copy(j, behind(j)).wait_recv()
    both = jnp.concatenate([t_all[q, pl.ds(0, N)] for q in range(NY)], axis=1)
    diag = jnp.concatenate([t_all[q, pl.ds(N, EXTRA)] for q in range(NY)], axis=1)[0:1]
    flip = both.T.astype(f32)
    both = both.astype(f32)
    l_old = jnp.where(row <= col, both, flip)
    r_old = jnp.where(row > col, both, flip)
    r_old = jnp.where(row == col, diag.astype(f32), r_old)
    hop(1, 0)
    for j in (1, 3, 2):
        for i in range(2):
            ga_copy(j, behind(j), i).wait_recv()
    hop(2, 0)
    hop(1, 1)
    h = jnp.concatenate([g_all[q].reshape(N, Q) for q in range(NY)], axis=1)
    xr = root(BETA * r_old + dot(h, h, 1, 1), eye)
    part = dot(xr, h, 1, 0).astype(bf16)
    xl_buf[...] = root(BETA * l_old + dot(h, h, 0, 0), eye)
    half = xl_buf[pl.ds(pl.multiple_of(lax.rem(y, 2) * TOK, TOK), TOK)]
    pre = dot(half, part, 1, 1).astype(bf16)
    pre_buf[...] = pre
    pf = pre.astype(f32)
    psum = jnp.sum(pf * pf, axis=(0, 1), keepdims=True)

    stages = [
        (NT, lambda j: (dp, ts[j])),
        (NY, lambda j: (ydp[j], t)),
        (NZ, lambda j: (zdp[j], t)),
    ]

    def s_copy(i, j):
        return remote(
            sums.at[i, 0], sums.at[i, j], s_send.at[i, j], s_recv.at[i, j], *stages[i][1](j)
        )

    def sum_start(i, value):
        sums[i, 0] = value
        for j in range(1, stages[i][0]):
            s_copy(i, j).start()

    def sum_end(i):
        for j in range(1, stages[i][0]):
            s_copy(i, j).wait_recv()
        return functools.reduce(jnp.add, [sums[i, j] for j in range(stages[i][0])])

    sum_start(0, jnp.stack([jnp.broadcast_to(v, (8, 128)) for v in (gsum, psum)]))
    hop(3, 0)
    hop(2, 1)
    sum_start(1, sum_end(0))
    hop(3, 1)
    sum_start(2, sum_end(1))
    to_owners(0)
    to_owners(1)
    total = sum_end(2)
    ratio = jnp.sqrt(total[0] / total[1])[0:1, 0:1]
    out_ref[...] = (pre_buf[...].astype(f32) * ratio).astype(bf16)

    for i in range(2):
        for j in (1, 3, 2):
            y_copy(j, behind(j), i).wait_recv()

    for j in (1, 2, 3):
        for s in range(SLOTS):
            t_copy(j, s, y).wait_send()
        o_copy(j).wait_send()
        ta_copy(j, y).wait_send()
        for i in range(2):
            ga_copy(j, y, i).wait_send()
        for i in range(2):
            y_copy(j, y, i).wait_send()
    for k in range(NZ):
        f_copy(k, core).wait_send()
        for j in (1, 2, 3):
            a_copy(k, j).wait_send()
        for d, s, p in moves_of(k):
            t_chain(d, s, p).wait_send()
            chain(d, s, p).wait_send()
            if s < 3 or p == d:
                for i in range(2):
                    g_copy(d, s, p, i).wait_send()
    for d in (RIGHT, LEFT):
        for i in range(2):
            g_copy(d, 0, 1 - d, i).wait_send()
    for i in range(3):
        for j in range(1, stages[i][0]):
            s_copy(i, j).wait_send()


def update_kernel(own_ref, slot_ref, h_ref, l_ref, r_ref, lo_ref, ro_ref):
    _, used = held(own_ref, slot_ref, lax.axis_index("dp"), pl.program_id(0))

    @pl.when(used == 0)
    def _():
        lo_ref[...] = l_ref[...]
        ro_ref[...] = r_ref[...]

    @pl.when(used != 0)
    def _():
        h = jnp.concatenate([h_ref[:, q, 0].reshape(N, Q) for q in range(NY)], axis=1)
        lo_ref[0] = BETA * l_ref[0] + dot(h, h, 0, 0)
        ro_ref[0] = BETA * r_ref[0] + dot(h, h, 1, 1)


def root(mat, eye):
    norm = jnp.sqrt(jnp.sum(mat * mat, axis=(0, 1), keepdims=True))
    scale = 2.5 / norm
    m = mat * scale
    mb = m.astype(bf16)
    square = dot(mb, mb, 1, 0)
    s2 = (1.5625 * eye - 0.625 * m + 0.0625 * square).astype(bf16)
    sm = (1.25 * m - 0.25 * square).astype(bf16)
    s4 = dot(s2, s2, 1, 0).astype(bf16)
    x = 1.5625 * eye - 0.3125 * m - 0.25 * dot(s4, sm, 1, 0)
    return (x * jnp.sqrt(jnp.sqrt(scale))).astype(bf16)


VMEM = pl.BlockSpec(memory_space=pltpu.VMEM)
SMEM = pl.BlockSpec(memory_space=pltpu.SMEM)
HBM = pl.BlockSpec(memory_space=pltpu.MemorySpace.HBM)
DMA = pltpu.SemaphoreType.DMA


def shards(activations, out_grads, owner, slot, left_state, right_state):
    direction, h = pl.pallas_call(
        step_kernel,
        out_shape=[
            jax.ShapeDtypeStruct((TOK, N), bf16),
            jax.ShapeDtypeStruct((2, NY, SLOTS, HALF, Q), bf16),
        ],
        in_specs=[HBM, VMEM, SMEM, SMEM, HBM, HBM],
        out_specs=[VMEM, VMEM],
        scratch_shapes=[
            pltpu.VMEM((SLOTS, N, N), f32),
            pltpu.VMEM((SLOTS, N, N), f32),
            pltpu.VMEM((NY, SLOTS, N + EXTRA, Q), bf16),
            pltpu.VMEM((NY, SLOTS, N + EXTRA, Q), bf16),
            pltpu.VMEM((2, 4, 2, N + EXTRA, Q), bf16),
            pltpu.VMEM((2, 4, 2, N + EXTRA, Q), bf16),
            pltpu.VMEM((2, N + EXTRA, Q), bf16),
            pltpu.VMEM((NY, N + EXTRA, Q), bf16),
            pltpu.VMEM((NZ, 2, NY, TOK, Q), bf16),
            pltpu.VMEM((NY, N, TOK), bf16),
            pltpu.VMEM((2, 4, 2, N, Q), bf16),
            pltpu.VMEM((2, 4, 2, N, Q), bf16),
            pltpu.VMEM((NBLK, HALF, Q), bf16),
            pltpu.VMEM((NBLK, HALF, Q), bf16),
            pltpu.VMEM((NY, 2, HALF, Q), bf16),
            pltpu.VMEM((2, NY, SLOTS, HALF, Q), bf16),
            pltpu.VMEM((N, N), bf16),
            pltpu.VMEM((TOK, N), bf16),
            pltpu.VMEM((3, NT, 2, 8, 128), f32),
            DMA((2, SLOTS)),
            DMA((NY, SLOTS)), DMA((NY, SLOTS)),
            DMA((2, 4, 2)), DMA((2, 4, 2)),
            DMA((NY,)), DMA((NY,)),
            DMA((NY,)), DMA((NY,)),
            DMA((NZ, 2)),
            DMA((NZ, NY)), DMA((NZ, NY)),
            DMA((NZ,)), DMA((NZ,)),
            DMA((2, 4, 2)), DMA((2, 4, 2)),
            DMA((2, 4, 2, 2)), DMA((2, 4, 2, 2)),
            DMA((NY, 2)), DMA((NY, 2)),
            DMA((2, NY)), DMA((2, NY)),
            DMA((3, NT)), DMA((3, NT)),
        ],
        compiler_params=pltpu.CompilerParams(
            collective_id=0, has_side_effects=True, vmem_limit_bytes=56 * 2**20
        ),
        name="step",
    )(
        activations, out_grads, owner, slot,
        left_state[0, 0], right_state[0, 0],
    )
    state = pl.BlockSpec((1, N, N), lambda s: (s, 0, 0))
    left_out, right_out = pl.pallas_call(
        update_kernel,
        grid=(SLOTS,),
        out_shape=[jax.ShapeDtypeStruct((SLOTS, N, N), f32)] * 2,
        in_specs=[
            SMEM, SMEM, pl.BlockSpec((2, NY, 1, HALF, Q), lambda s: (0, 0, s, 0, 0)), state, state,
        ],
        out_specs=[state, state],
        compiler_params=pltpu.CompilerParams(vmem_limit_bytes=24 * 2**20),
        name="update",
    )(owner, slot, h, left_state[0, 0], right_state[0, 0])
    return direction, left_out[None, None], right_out[None, None]


def solution(mesh):
    return jax.shard_map(
        shards,
        mesh=mesh,
        in_specs=(
            P("dp", None),
            P("dp", "tensor"),
            P("tensor", None),
            P("tensor", None),
            P("tensor", "dp", None, None, None),
            P("tensor", "dp", None, None, None),
        ),
        out_specs=(
            P("dp", "tensor"),
            P("tensor", "dp", None, None, None),
            P("tensor", "dp", None, None, None),
        ),
        check_vma=False,
    )
```

```python
import functools

import jax
import jax.numpy as jnp
from jax import lax
from jax.experimental import pallas as pl
from jax.experimental.pallas import tpu as pltpu
from jax.sharding import PartitionSpec as P

N = 512
HALF = 256
Q = 128
NZ, NY, NX, NT = 8, 4, 4, 8
SLOTS, NBLK, TOK = 2, 16, 256
XTOK = TOK // NX
EXTRA = 16
BETA = 0.95
MESH = pl.DeviceIdType.MESH
RIGHT, LEFT = 0, 1
bf16, f32 = jnp.bfloat16, jnp.float32


def place():
    dp, t = lax.axis_index("dp"), lax.axis_index("tensor")
    return dp, t, dp // NY, lax.rem(dp, NY)


def ring(z, step):
    return lax.rem(z + step + NZ, NZ)


def remote(src, dst, send, recv, dp, t):
    return pltpu.make_async_remote_copy(
        src_ref=src, dst_ref=dst, send_sem=send, recv_sem=recv,
        device_id=(dp, t), device_id_type=MESH,
    )


def dot(a, b, ca, cb):
    return lax.dot_general(a, b, (((ca,), (cb,)), ((), ())), preferred_element_type=f32)


def held(own_ref, slot_ref, device, slot):
    block, used = jnp.int32(0), jnp.int32(0)
    for b in range(NBLK):
        hit = (own_ref[0, b] == device) & (slot_ref[0, b] == slot)
        block = jnp.where(hit, b, block)
        used = jnp.where(hit, 1, used)
    return block, used


def chunk_of(z, k):
    far = 4 - (k + 1) // 2
    return ring(z, far if k % 2 else -far)


def moves_of(k):
    if k == 0:
        return [(RIGHT, 0, 0), (LEFT, 0, 1)]
    if k == NZ - 1:
        return []
    return [((RIGHT if k % 2 else LEFT), (k + 1) // 2, p) for p in range(2)]


def step_kernel(
    a_ref, o_ref, own_ref, slot_ref, l_ref, r_ref, out_ref, h_ref,
    l_buf, r_buf, tp, got, t_snd, t_rcv, t_fin, t_all,
    a_buf, o_buf, ot_buf, snd, rcv, gath_0, gath_1, g_all, stage, xl_buf, pre_buf, sums,
    st_sem, t_send, t_recv, c_send, c_recv, ta_send, ta_recv,
    o_send, o_recv, own_sem, a_send, a_recv, x_send, x_recv, f_send, f_recv,
    r_send, r_recv, g_send, g_recv, ga_send, ga_recv, y_send, y_recv, s_send, s_recv,
):
    dp, t, z, y = place()
    core, x = lax.rem(t, 2), t // 2
    low = lax.rem(x, 2)
    xt = [2 * lax.rem(x + i, NX) + core for i in (1, NX - 1)]
    gath = (gath_0, gath_1)
    twin = t + 1 - 2 * core
    ys = [lax.rem(y + j, NY) for j in range(NY)]
    ydp = [z * NY + yj for yj in ys]
    side = [ring(z, 1) * NY + y, ring(z, -1) * NY + y]
    ts = [lax.rem(t + j, NT) for j in range(NT)]
    zdp = [ring(z, j) * NY + y for j in range(NZ)]

    def behind(j):
        return ys[(NY - j) % NY]

    def columns(c, p, yj):
        return pl.ds(pl.multiple_of((2 * c + p) * N + yj * Q, Q), Q)

    state_in = [
        pltpu.make_async_copy(ref.at[s], buf.at[s], st_sem.at[i, s])
        for s in range(SLOTS)
        for i, (ref, buf) in enumerate(((l_ref, l_buf), (r_ref, r_buf)))
    ]
    for copy in state_in:
        copy.start()
    peers = (
        [(ydp[j], t) for j in range(1, NY)]
        + [(dp, ts[j]) for j in range(1, NT)]
        + [(zdp[j], t) for j in range(1, NZ)]
    )
    met = pltpu.get_barrier_semaphore()
    for peer in peers:
        pl.semaphore_signal(met, inc=1, device_id=peer, device_id_type=MESH)

    def own_copy(k, p):
        c = chunk_of(z, k)
        return pltpu.make_async_copy(
            a_ref.at[:, :, :, columns(c, p, y)], a_buf.at[c, p, :, :, 0], own_sem.at[k, p]
        )

    for k in range(NZ):
        for p in range(2):
            own_copy(k, p).start()
    o_buf[:, :, 0] = o_ref[...]

    row = lax.broadcasted_iota(jnp.int32, (N, N), 0)
    col = lax.broadcasted_iota(jnp.int32, (N, N), 1)
    def t_copy(j, s, src):
        return remote(
            tp.at[ys[j], s], got.at[src, s], t_send.at[j, s], t_recv.at[j, s], ydp[j], t
        )

    for s in range(SLOTS):
        for copy in state_in[2 * s : 2 * s + 2]:
            copy.wait()
        both = jnp.where(row <= col, l_buf[s], r_buf[s]).astype(bf16)
        diag = jnp.sum(jnp.where(row == col, r_buf[s], 0.0), axis=0, keepdims=True)
        diag = jnp.broadcast_to(diag, (EXTRA, N)).astype(bf16)
        for q in range(NY):
            tp[q, s, pl.ds(0, N)] = both[:, q * Q : (q + 1) * Q]
            tp[q, s, pl.ds(N, EXTRA)] = diag[:, q * Q : (q + 1) * Q]
        if s == 0:
            pl.semaphore_wait(met, len(peers))
        for j in (2, 1, 3):
            t_copy(j, s, y).start()

    def o_copy(j):
        return remote(o_ref, o_buf.at[:, :, j], o_send.at[j], o_recv.at[j], ydp[j], t)

    def a_copy(k, j):
        c = chunk_of(z, k)
        return remote(
            a_ref.at[:, low, :, columns(c, core, ys[j])], a_buf.at[c, core, :, low, j],
            a_send.at[k, j], a_recv.at[k, j], ydp[j], t,
        )

    def x_copy(k, i, parity):
        part = a_buf.at[chunk_of(z, k), core, i, parity, 1:]
        return remote(part, part, x_send.at[k, i], x_recv.at[k, i], dp, xt[i])

    def f_copy(k, p):
        part = a_buf.at[chunk_of(z, k), p, :, :, 1:]
        return remote(part, part, f_send.at[k], f_recv.at[k], dp, twin)

    def along_x(k):
        for j in (1, 3, 2):
            a_copy(k, j).wait_recv()
        for i in range(2):
            x_copy(k, i, low).start()

    def to_twin(k):
        for i in range(2):
            x_copy(k, i, 1 - low).wait_recv()
        f_copy(k, core).start()

    for k in range(NZ):
        for j in (2, 1, 3):
            a_copy(k, j).start()
    for j in (2, 1, 3):
        o_copy(j).start()
    got[y] = tp[y]

    def t_chain(d, s, p):
        return remote(
            t_snd.at[d, s, p], t_rcv.at[d, s, p], c_send.at[d, s, p], c_recv.at[d, s, p], side[d], t
        )

    def place_of(c, p):
        owner = own_ref[0, 2 * c + p]
        return owner // NY, lax.rem(owner, NY), slot_ref[0, 2 * c + p]

    for s in range(SLOTS):
        for j in (1, 3, 2):
            t_copy(j, s, behind(j)).wait_recv()
    for k in range(NZ):
        for d, s, p in moves_of(k):
            oz, oy, os = place_of(chunk_of(z, k), p)
            value = got[oy, os]
            if s > 1 or (s == 1 and p == d):
                t_chain(d, s - 1, p).wait_recv()
                value = jnp.where(oz == z, value, t_rcv[d, s - 1, p])
            t_snd[d, s, p] = value
            t_chain(d, s, p).start()
        along_x(k)
    for p in range(2):
        oz, oy, os = place_of(z, p)
        for d in (RIGHT, LEFT):
            t_chain(d, 3, p).wait_recv()
        back = ring(z, -oz)
        from_left = (back < 4) | ((back == 4) & (p == 0))
        value = jnp.where(from_left, t_rcv[RIGHT, 3, p], t_rcv[LEFT, 3, p])
        t_fin[p] = jnp.where(oz == z, got[oy, os], value)

    def ta_copy(j, src):
        return remote(t_fin.at[ys[j] // 2], t_all.at[src], ta_send.at[j], ta_recv.at[j], ydp[j], t)

    def ga_copy(j, src, i):
        piece = gath[i].at[2 * z + ys[j] // 2]
        return remote(piece, g_all.at[src, i], ga_send.at[j, i], ga_recv.at[j, i], ydp[j], t)

    for j in (2, 1, 3):
        ta_copy(j, y).start()
    t_all[y] = t_fin[y // 2]

    def chain(d, s, p):
        return remote(
            snd.at[d, s, p], rcv.at[d, s, p], r_send.at[d, s, p], r_recv.at[d, s, p], side[d], t
        )

    for j in (1, 3, 2):
        o_copy(j).wait_recv()
    to_twin(0)
    ot_buf[...] = o_buf[...].reshape(NY * TOK, N).T
    to_twin(1)
    for k in range(NZ):
        c = chunk_of(z, k)
        if k + 2 < NZ:
            to_twin(k + 2)
        for p in range(2):
            own_copy(k, p).wait()
        f_copy(k, 1 - core).wait_recv()
        acts = jnp.concatenate([a_buf[c, p].reshape(NY * TOK, Q) for p in range(2)], axis=1)
        part = dot(ot_buf[...], acts, 1, 0)
        part = [part[:, :Q], part[:, Q:]]
        for d, s, p in moves_of(k):
            value = part[p]
            if s > 1 or (s == 1 and p == d):
                chain(d, s - 1, p).wait_recv()
                value = value + rcv[d, s - 1, p].astype(f32)
            snd[d, s, p] = value.astype(bf16)
            chain(d, s, p).start()
    gsum = jnp.zeros((1, 1), f32)
    for p in range(2):
        for d in (RIGHT, LEFT):
            chain(d, 3, p).wait_recv()
        total = part[p] + rcv[RIGHT, 3, p].astype(f32) + rcv[LEFT, 3, p].astype(f32)
        total = total.astype(bf16)
        for i in range(2):
            gath[i][2 * z + p] = total[i * HALF : (i + 1) * HALF]
        total = total.astype(f32)
        gsum = gsum + jnp.sum(total * total, axis=(0, 1), keepdims=True)

    def g_copy(d, s, p, i):
        piece = gath[i].at[2 * ring(z, -s if d == RIGHT else s) + p]
        return remote(piece, piece, g_send.at[d, s, p, i], g_recv.at[d, s, p, i], side[d], t)

    def g_wait(d, s, p, i):
        piece = gath[i].at[2 * ring(z, -s - 1 if d == RIGHT else s + 1) + p]
        remote(
            piece, piece, g_send.at[d, s, p, i], g_recv.at[d, s, p, i], side[d], t
        ).wait_recv()

    def hop(s, i):
        for p in range(2):
            for d in (RIGHT, LEFT):
                if s < 3 or p == d:
                    if s > 0:
                        g_wait(d, s - 1, p, i)
                    g_copy(d, s, p, i).start()

    def y_copy(j, src, i):
        return remote(
            stage.at[i, j], h_ref.at[i, src], y_send.at[i, j], y_recv.at[i, j], ydp[j], t
        )

    picks = [[held(own_ref, slot_ref, ydp[j], s)[0] for s in range(SLOTS)] for j in range(NY)]

    def to_owners(i):
        for d in (RIGHT, LEFT):
            g_wait(d, 2, 1 - d, i)
            g_wait(d, 3, d, i)
        for j in (2, 1, 3, 0):
            for s in range(SLOTS):
                if j:
                    stage[i, j, s] = gath[i][picks[j][s]]
                else:
                    h_ref[i, y, s] = gath[i][picks[j][s]]
            if j:
                y_copy(j, y, i).start()

    hop(0, 0)
    hop(0, 1)
    for j in (2, 1, 3):
        for i in range(2):
            ga_copy(j, y, i).start()
    for i in range(2):
        g_all[y, i] = gath[i][2 * z + y // 2]

    eye = (row == col).astype(f32)
    for j in (1, 3, 2):
        ta_copy(j, behind(j)).wait_recv()
    both = jnp.concatenate([t_all[q, pl.ds(0, N)] for q in range(NY)], axis=1)
    diag = jnp.concatenate([t_all[q, pl.ds(N, EXTRA)] for q in range(NY)], axis=1)[0:1]
    flip = both.T.astype(f32)
    both = both.astype(f32)
    l_old = jnp.where(row <= col, both, flip)
    r_old = jnp.where(row > col, both, flip)
    r_old = jnp.where(row == col, diag.astype(f32), r_old)
    hop(1, 0)
    for j in (1, 3, 2):
        for i in range(2):
            ga_copy(j, behind(j), i).wait_recv()
    hop(2, 0)
    hop(1, 1)
    h = jnp.concatenate([g_all[q].reshape(N, Q) for q in range(NY)], axis=1)
    xr = root(BETA * r_old + dot(h, h, 1, 1), eye)
    part = dot(xr, h, 1, 0).astype(bf16)
    xl_buf[...] = root(BETA * l_old + dot(h, h, 0, 0), eye)
    half = xl_buf[pl.ds(pl.multiple_of(lax.rem(y, 2) * TOK, TOK), TOK)]
    pre = dot(half, part, 1, 1).astype(bf16)
    pre_buf[...] = pre
    pf = pre.astype(f32)
    psum = jnp.sum(pf * pf, axis=(0, 1), keepdims=True)

    stages = [
        (NT, lambda j: (dp, ts[j])),
        (NY, lambda j: (ydp[j], t)),
        (NZ, lambda j: (zdp[j], t)),
    ]

    def s_copy(i, j):
        return remote(
            sums.at[i, 0], sums.at[i, j], s_send.at[i, j], s_recv.at[i, j], *stages[i][1](j)
        )

    def sum_start(i, value):
        sums[i, 0] = value
        for j in range(1, stages[i][0]):
            s_copy(i, j).start()

    def sum_end(i):
        for j in range(1, stages[i][0]):
            s_copy(i, j).wait_recv()
        return functools.reduce(jnp.add, [sums[i, j] for j in range(stages[i][0])])

    sum_start(0, jnp.stack([jnp.broadcast_to(v, (8, 128)) for v in (gsum, psum)]))
    hop(3, 0)
    hop(2, 1)
    sum_start(1, sum_end(0))
    hop(3, 1)
    to_owners(0)
    sum_start(2, sum_end(1))
    to_owners(1)
    total = sum_end(2)
    ratio = jnp.sqrt(total[0] / total[1])[0:1, 0:1]
    out_ref[...] = (pre_buf[...].astype(f32) * ratio).astype(bf16)

    for i in range(2):
        for j in (1, 3, 2):
            y_copy(j, behind(j), i).wait_recv()

    for j in (1, 2, 3):
        for s in range(SLOTS):
            t_copy(j, s, y).wait_send()
        o_copy(j).wait_send()
        ta_copy(j, y).wait_send()
        for i in range(2):
            ga_copy(j, y, i).wait_send()
        for i in range(2):
            y_copy(j, y, i).wait_send()
    for k in range(NZ):
        f_copy(k, core).wait_send()
        for i in range(2):
            x_copy(k, i, low).wait_send()
        for j in (1, 2, 3):
            a_copy(k, j).wait_send()
        for d, s, p in moves_of(k):
            t_chain(d, s, p).wait_send()
            chain(d, s, p).wait_send()
            if s < 3 or p == d:
                for i in range(2):
                    g_copy(d, s, p, i).wait_send()
    for d in (RIGHT, LEFT):
        for i in range(2):
            g_copy(d, 0, 1 - d, i).wait_send()
    for i in range(3):
        for j in range(1, stages[i][0]):
            s_copy(i, j).wait_send()


def update_kernel(own_ref, slot_ref, h_ref, l_ref, r_ref, lo_ref, ro_ref):
    _, used = held(own_ref, slot_ref, lax.axis_index("dp"), pl.program_id(0))

    @pl.when(used == 0)
    def _():
        lo_ref[...] = l_ref[...]
        ro_ref[...] = r_ref[...]

    @pl.when(used != 0)
    def _():
        h = jnp.concatenate([h_ref[:, q, 0].reshape(N, Q) for q in range(NY)], axis=1)
        lo_ref[0] = BETA * l_ref[0] + dot(h, h, 0, 0)
        ro_ref[0] = BETA * r_ref[0] + dot(h, h, 1, 1)


def root(mat, eye):
    norm = jnp.sqrt(jnp.sum(mat * mat, axis=(0, 1), keepdims=True))
    scale = 2.5 / norm
    m = mat * scale
    mb = m.astype(bf16)
    square = dot(mb, mb, 1, 0)
    s2 = (1.5625 * eye - 0.625 * m + 0.0625 * square).astype(bf16)
    sm = (1.25 * m - 0.25 * square).astype(bf16)
    s4 = dot(s2, s2, 1, 0).astype(bf16)
    x = 1.5625 * eye - 0.3125 * m - 0.25 * dot(s4, sm, 1, 0)
    return (x * jnp.sqrt(jnp.sqrt(scale))).astype(bf16)


VMEM = pl.BlockSpec(memory_space=pltpu.VMEM)
SMEM = pl.BlockSpec(memory_space=pltpu.SMEM)
HBM = pl.BlockSpec(memory_space=pltpu.MemorySpace.HBM)
DMA = pltpu.SemaphoreType.DMA


def shards(activations, out_grads, owner, slot, left_state, right_state):
    direction, h = pl.pallas_call(
        step_kernel,
        out_shape=[
            jax.ShapeDtypeStruct((TOK, N), bf16),
            jax.ShapeDtypeStruct((2, NY, SLOTS, HALF, Q), bf16),
        ],
        in_specs=[HBM, VMEM, SMEM, SMEM, HBM, HBM],
        out_specs=[VMEM, VMEM],
        scratch_shapes=[
            pltpu.VMEM((SLOTS, N, N), f32),
            pltpu.VMEM((SLOTS, N, N), f32),
            pltpu.VMEM((NY, SLOTS, N + EXTRA, Q), bf16),
            pltpu.VMEM((NY, SLOTS, N + EXTRA, Q), bf16),
            pltpu.VMEM((2, 4, 2, N + EXTRA, Q), bf16),
            pltpu.VMEM((2, 4, 2, N + EXTRA, Q), bf16),
            pltpu.VMEM((2, N + EXTRA, Q), bf16),
            pltpu.VMEM((NY, N + EXTRA, Q), bf16),
            pltpu.VMEM((NZ, 2, 2, 2, NY, XTOK, Q), bf16),
            pltpu.VMEM((2, 2, NY, XTOK, N), bf16),
            pltpu.VMEM((N, NY * TOK), bf16),
            pltpu.VMEM((2, 4, 2, N, Q), bf16),
            pltpu.VMEM((2, 4, 2, N, Q), bf16),
            pltpu.VMEM((NBLK, HALF, Q), bf16),
            pltpu.VMEM((NBLK, HALF, Q), bf16),
            pltpu.VMEM((NY, 2, HALF, Q), bf16),
            pltpu.VMEM((2, NY, SLOTS, HALF, Q), bf16),
            pltpu.VMEM((N, N), bf16),
            pltpu.VMEM((TOK, N), bf16),
            pltpu.VMEM((3, NT, 2, 8, 128), f32),
            DMA((2, SLOTS)),
            DMA((NY, SLOTS)), DMA((NY, SLOTS)),
            DMA((2, 4, 2)), DMA((2, 4, 2)),
            DMA((NY,)), DMA((NY,)),
            DMA((NY,)), DMA((NY,)),
            DMA((NZ, 2)),
            DMA((NZ, NY)), DMA((NZ, NY)),
            DMA((NZ, 2)), DMA((NZ, 2)),
            DMA((NZ,)), DMA((NZ,)),
            DMA((2, 4, 2)), DMA((2, 4, 2)),
            DMA((2, 4, 2, 2)), DMA((2, 4, 2, 2)),
            DMA((NY, 2)), DMA((NY, 2)),
            DMA((2, NY)), DMA((2, NY)),
            DMA((3, NT)), DMA((3, NT)),
        ],
        compiler_params=pltpu.CompilerParams(
            collective_id=0, has_side_effects=True, vmem_limit_bytes=56 * 2**20
        ),
        name="step",
    )(
        activations.reshape(2, 2, XTOK, -1), out_grads.reshape(2, 2, XTOK, N), owner, slot,
        left_state[0, 0], right_state[0, 0],
    )
    state = pl.BlockSpec((1, N, N), lambda s: (s, 0, 0))
    left_out, right_out = pl.pallas_call(
        update_kernel,
        grid=(SLOTS,),
        out_shape=[jax.ShapeDtypeStruct((SLOTS, N, N), f32)] * 2,
        in_specs=[
            SMEM, SMEM, pl.BlockSpec((2, NY, 1, HALF, Q), lambda s: (0, 0, s, 0, 0)), state, state,
        ],
        out_specs=[state, state],
        compiler_params=pltpu.CompilerParams(vmem_limit_bytes=24 * 2**20),
        name="update",
    )(owner, slot, h, left_state[0, 0], right_state[0, 0])
    return direction, left_out[None, None], right_out[None, None]


def solution(mesh):
    return jax.shard_map(
        shards,
        mesh=mesh,
        in_specs=(
            P("dp", None),
            P("dp", "tensor"),
            P("tensor", None),
            P("tensor", None),
            P("tensor", "dp", None, None, None),
            P("tensor", "dp", None, None, None),
        ),
        out_specs=(
            P("dp", "tensor"),
            P("tensor", "dp", None, None, None),
            P("tensor", "dp", None, None, None),
        ),
        check_vma=False,
    )
```
